512 devices in a mesh: mp: 128 (over x, y_hi, z, core), tok: 4 (over y_lo).
Axes of the slice: x: 4, y: 8 (y_hi: 2, y_lo: 4; y = y_hi * 4 + y_lo), z: 8, core: 2. Of those that a mesh axis runs over, the one named last changes fastest.
Arguments:
- tokens: bfloat16 [896, 4096], P('tok'), may hold values from -6 to 6
- gate_weight: bfloat16 [49152, 4096], P('mp', 'tok'), may hold values from -6 to 6
- up_weight: bfloat16 [49152, 4096], P('mp', 'tok'), may hold values from -6 to 6
- pair_list: int32 [16], replicated, may hold values from 0 to 15, each once
- unit_perm: int32 [16, 1536], replicated, may hold values from 0 to 1535, each once within a row
Outputs:
- merged_gate: bfloat16 [49152, 4096], P('mp', 'tok')
- merged_up: bfloat16 [49152, 4096], P('mp', 'tok')
- correlation: bfloat16 [49152, 768], P('mp', 'tok')
The draws below stay inside these ranges and needn't reach their ends.
Inputs may be any that keep to these rules, and one draw needn't show every extreme that they name: pair_list is a permutation of the 16 slots. Each row of unit_perm is a permutation of the 1536 hidden units.
All inputs are finite; a program needn't handle non-finite values.
Results may differ from the reference program's by a relative error of at most 0.0057.
Values may be sent and summed in bfloat16 or wider, within the bound.
A program may use at most 64 MiB of HBM per device.

```python
import jax
import jax.numpy as jnp
from jax import lax

D = 4096
FF = 1536
PAIRS = 16
TOKENS = 896


def levels(own_key, extent, shards, smallest, high):
    factor_of = 1.0
    for axis_at, parts in shards:
        steps = jax.random.uniform(jax.random.fold_in(jax.random.fold_in(own_key, 6), axis_at), (parts,), jnp.float32, smallest / len(shards), high / len(shards))
        factor_of = factor_of * jnp.repeat(jnp.exp(steps), extent[axis_at] // parts).reshape((-1,) + (1,) * (len(extent) - 1 - axis_at))
    return factor_of


def bell_draw(rng, extent, deviation, most, cuts=(), kind=jnp.bfloat16):
    entries = deviation * jax.random.normal(rng, extent, jnp.float32)
    if cuts:
        entries = entries * levels(rng, extent, cuts, -0.22, 0.18)
    return jnp.clip(entries, -most, most).astype(kind)


def setup_inputs(seed: int = 0) -> dict:
    seeds = jax.random.split(jax.random.key(seed), 6)
    tokens = bell_draw(seeds[0], (TOKENS, D), 1.0, 6.0, ((0, 4),))
    gate_weight = bell_draw(seeds[1], (2 * PAIRS * FF, D), 1.0, 6.0, ((0, 128), (1, 4)))
    up_weight = bell_draw(seeds[2], (2 * PAIRS * FF, D), 1.0, 6.0, ((0, 128), (1, 4)))
    pair_list = jax.random.permutation(seeds[3], PAIRS).astype(jnp.int32)
    unit_perm = jax.vmap(lambda own: jax.random.permutation(own, FF))(jax.random.split(seeds[4], PAIRS)).reshape((PAIRS, FF)).astype(jnp.int32)
    return dict(tokens=tokens, gate_weight=gate_weight, up_weight=up_weight, pair_list=pair_list, unit_perm=unit_perm)


def swiglu_hidden(tokens, gate_rows, up_rows):
    scale = D ** -0.5
    gate_part = jnp.dot(tokens, gate_rows.T, preferred_element_type=jnp.float32) * scale
    up_part = jnp.dot(tokens, up_rows.T, preferred_element_type=jnp.float32) * scale
    return (jax.nn.silu(gate_part) * up_part).astype(jnp.bfloat16)


def reference(tokens, gate_weight, up_weight, pair_list, unit_perm):
    gate_split = gate_weight.reshape(2, PAIRS, FF, D)
    up_split = up_weight.reshape(2, PAIRS, FF, D)
    slot_ids = jnp.arange(PAIRS, dtype=jnp.int32)
    inverse_pairs = jnp.zeros((PAIRS,), jnp.int32).at[pair_list].set(slot_ids)
    unit_ids = jnp.arange(FF, dtype=jnp.int32)

    def cross_of(slot_index):
        partner_slot = pair_list[slot_index]
        first_hidden = swiglu_hidden(tokens, gate_split[0, slot_index], up_split[0, slot_index])
        second_hidden = swiglu_hidden(tokens, gate_split[1, partner_slot], up_split[1, partner_slot])
        return jnp.dot(first_hidden.T, second_hidden, preferred_element_type=jnp.float32) * TOKENS ** -0.5

    cross = lax.map(cross_of, slot_ids)

    def merge_of(slot_index):
        partner_slot = pair_list[slot_index]
        order = unit_perm[slot_index]
        mid_gate = ((gate_split[0, slot_index].astype(jnp.float32) + gate_split[1, partner_slot][order].astype(jnp.float32)) * 0.5).astype(jnp.bfloat16)
        mid_up = ((up_split[0, slot_index].astype(jnp.float32) + up_split[1, partner_slot][order].astype(jnp.float32)) * 0.5).astype(jnp.bfloat16)
        first_slot = inverse_pairs[slot_index]
        back_order = jnp.zeros((FF,), jnp.int32).at[unit_perm[first_slot]].set(unit_ids)
        diff_gate = ((gate_split[1, slot_index].astype(jnp.float32) - gate_split[0, first_slot][back_order].astype(jnp.float32)) * 0.5).astype(jnp.bfloat16)
        diff_up = ((up_split[1, slot_index].astype(jnp.float32) - up_split[0, first_slot][back_order].astype(jnp.float32)) * 0.5).astype(jnp.bfloat16)
        return mid_gate, mid_up, diff_gate, diff_up

    mid_gate, mid_up, diff_gate, diff_up = lax.map(merge_of, slot_ids)
    merged_gate = jnp.concatenate([mid_gate, diff_gate], axis=0).reshape(2 * PAIRS * FF, D)
    merged_up = jnp.concatenate([mid_up, diff_up], axis=0).reshape(2 * PAIRS * FF, D)
    upper = cross[:, :, : FF // 2]
    lower = cross[inverse_pairs][:, :, FF // 2:]
    correlation = jnp.concatenate([upper, lower], axis=0).reshape(2 * PAIRS * FF, FF // 2).astype(jnp.bfloat16)
    return merged_gate, merged_up, correlation
```

```python
import functools

import jax
import jax.numpy as jnp
from jax import lax
from jax.experimental import pallas as pl
from jax.experimental.pallas import tpu as pltpu
from jax.sharding import PartitionSpec as P

GROUP = 4
TOK = 4
MESH = pl.DeviceIdType.MESH
BF16 = jnp.bfloat16
F32 = jnp.float32


def kernel(
    gate_ref, up_ref, tokens_ref, row_ref, col_ref, table_ref,
    fetched_ref, corr_ref,
    onehot, gathered, ordered, spread_gate, spread_up, chosen,
    tok_cols, part_send, part_own, part_recv, hidden, hid_spread, hid_chosen, row_units, col_units,
    tok_send, tok_recv, core_send, core_recv, pe_send, pe_recv,
    one_send, one_recv, two_send, two_recv, rs_send, rs_recv,
    own_send, own_recv, h1_send, h1_recv, h2_send, h2_recv,
):
    mp = lax.axis_index("mp")
    tok = lax.axis_index("tok")
    spread = (spread_gate, spread_up)
    slots, chunk, width = spread_gate.shape
    rows = gate_ref.shape[0]
    per_piece = slots // GROUP
    model = mp // (slots * GROUP)
    slot = (mp // GROUP) % slots
    piece = mp % GROUP
    core = mp % 2
    y_hi = (mp // 16) % 2
    flipped = mp + 16 * (1 - 2 * y_hi)
    part = hidden.shape[0]
    lanes = hidden.shape[1]
    hid_rows, hid_lanes = hid_spread.shape[1:]
    across = lanes // hid_lanes
    hid_chunks = across * (part // hid_rows)

    def device(m, s, p):
        return (m * slots + s) * GROUP + p

    def along_y(step):
        there = tok + step
        wraps = jnp.logical_or(there < 0, there >= TOK)
        return jnp.where(wraps, flipped, mp), lax.rem(there + TOK, TOK)

    def remote(src, dst, send, recv, who):
        return pltpu.make_async_remote_copy(
            src_ref=src, dst_ref=dst, send_sem=send, recv_sem=recv, device_id=who, device_id_type=MESH
        )

    def arrived(dst, recv):
        remote(dst, dst, recv, recv, (mp, tok)).wait_recv()

    def left(src, send):
        remote(src, src, send, send, (mp, tok)).wait_send()

    def loop(count, fn):
        lax.fori_loop(0, count, lambda i, c: (fn(i), c)[1], 0)

    barrier = pltpu.get_barrier_semaphore()

    def greet(who):
        pl.semaphore_signal(barrier, inc=1, device_id=who, device_id_type=MESH)

    far = jnp.where(core == 1, 2, -2)
    greet(along_y(-1))
    greet(along_y(1))
    greet(along_y(-far))
    for d in range(1, GROUP):
        greet((device(model, slot, lax.rem(piece + d, GROUP)), tok))
    for d in range(1, TOK):
        greet((mp, lax.rem(tok + d, TOK)))

    def greet_relays(d):
        s = lax.rem(slot + d, slots)

        @pl.when(d > 0)
        def _():
            greet((device(model, s, piece), tok))

        greet((device(1 - model, s, piece), tok))

    loop(slots, greet_relays)

    def greet_two(i):
        k = piece * per_piece + i // GROUP
        c = lax.rem(i, GROUP)
        greet((device(1 - model, k, c), tok))

        @pl.when(jnp.logical_or(k != slot, c != piece))
        def _():
            greet((device(model, k, c), tok))

    loop(slots, greet_two)

    first_col = 2 * lax.rem(tok, 2)

    @pl.when(model == 1)
    def _():
        loop(
            hid_chunks,
            lambda k: [greet((device(0, k, piece), t)) for t in range(TOK)],
        )
        for i in range(2):

            @pl.when(jnp.logical_or(piece != 2 + tok // 2, tok != first_col + i))
            def _():
                greet((device(1, slot, 2 + tok // 2), first_col + i))

    @pl.when(model == 0)
    def _():
        loop(
            hid_chunks,
            lambda k: [greet((device(0 + 1, k, tok // 2), first_col + i)) for i in range(2)],
        )

    forward = model == 1
    block = 128
    lane_id = lax.broadcasted_iota(jnp.int32, (1, onehot.shape[1]), 1)
    right = jnp.where(forward, lane_id, row_ref[...])

    def fill(i):
        at = pl.ds(pl.multiple_of(i * block, block), block)
        unit_id = lax.broadcasted_iota(jnp.int32, (block, 1), 0) + i * block
        lhs = jnp.where(forward, col_ref[at, :], unit_id)
        onehot[at, :] = jnp.where(lhs == right, 1.0, 0.0).astype(BF16)

    loop(onehot.shape[0] // block, fill)

    relays_hidden = slot < hid_chunks
    sends_two = jnp.logical_and(relays_hidden, jnp.logical_or(model == 0, piece < 2))
    to_self_two = slot // per_piece == piece
    late_tok = lax.rem(piece * TOK + tok, 2 * TOK) // 2
    own_to_self = late_tok == tok
    expected = 3 + (GROUP - 1) + (TOK - 1) + (slots - 1) + slots + slots
    expected = expected + slots - jnp.where(to_self_two, 1, 0)
    expected = expected + jnp.where(sends_two, slots * 4, 0)
    expected = expected + jnp.where(
        jnp.logical_and(model == 1, piece >= 2), jnp.where(own_to_self, 3, 4), 0
    )
    pl.semaphore_wait(barrier, expected)

    tok_rows = tokens_ref.shape[0]
    half_rows = pl.ds(pl.multiple_of(core * (tok_rows // 2), 16), tok_rows // 2)
    model_cols = gate_ref.shape[1]

    def cols_of(t):
        return pl.ds(pl.multiple_of(t * model_cols, 128), model_cols)

    for i, step in enumerate((1, -1, far)):
        who = along_y(step)
        remote(
            tokens_ref.at[half_rows, cols_of(who[1])], tok_cols.at[tok, half_rows, :],
            tok_send.at[i], tok_recv.at[i], who,
        ).start()

    weights = (gate_ref, up_ref)
    own_rows = pl.ds(pl.multiple_of(piece * rows, 128), rows)

    def width_of(c):
        return pl.ds(pl.multiple_of(c * width, 128), width)

    for a in range(2):
        for d in range(1, GROUP):
            c = lax.rem(piece + d, GROUP)
            remote(
                weights[a].at[:, width_of(c)], gathered.at[a, own_rows, :],
                pe_send.at[a, d], pe_recv.at[a, d], (device(model, slot, c), tok),
            ).start()
    for a in range(2):
        gathered[a, own_rows, :] = weights[a][:, width_of(piece)]
    tok_cols[tok] = tokens_ref[:, cols_of(tok)]

    def relay_side(a):
        return model if a == 0 else 1 - model

    def leg_one(a):
        for d in range(1, GROUP):
            arrived(gathered.at[a, pl.ds(0, rows), :], pe_recv.at[a, d])
        step = 2 * 192

        def order(i):
            at = pl.ds(pl.multiple_of(i * step, step), step)
            ordered[a, at, :] = jnp.dot(
                onehot[at, :], gathered[a], preferred_element_type=F32
            ).astype(BF16)

        loop(onehot.shape[0] // step, order)

        def send(d):
            k = lax.rem(slot + d, slots)
            at = pl.ds(pl.multiple_of(k * chunk, 16), chunk)

            def go():
                remote(
                    ordered.at[a, at, :], spread[a].at[slot],
                    one_send.at[a, d], one_recv.at[a, slot], (device(relay_side(a), k, piece), tok),
                ).start()

            if a == 0:
                pl.when(d > 0)(go)
            else:
                go()

        loop(slots, send)
        if a == 0:
            spread[a][slot] = ordered[a, pl.ds(pl.multiple_of(slot * chunk, 16), chunk), :]

    def leg_two(a):
        def come(s):
            def go():
                arrived(spread[a].at[0], one_recv.at[a, s])

            if a == 0:
                pl.when(s != slot)(go)
            else:
                go()

        loop(slots, come)
        side = relay_side(a)

        def select(t):
            chosen[a, t] = spread[a][table_ref[side, t]]

        loop(slots, select)
        mine = pl.ds(pl.multiple_of(lax.rem(slot, per_piece) * chunk, 16), chunk)
        target_piece = slot // per_piece

        def send(d):
            t = lax.rem(slot + d, slots)

            def go():
                remote(
                    chosen.at[a, t], fetched_ref.at[a, mine, width_of(piece)],
                    two_send.at[a, d], two_recv.at[a, lax.rem(slot, per_piece) * GROUP + piece],
                    (device(1 - side, t, target_piece), tok),
                ).start()

            if a == 0:
                go()
            else:
                same = jnp.logical_and(d == 0, to_self_two)
                pl.when(jnp.logical_not(same))(go)

                @pl.when(same)
                def _():
                    fetched_ref[a, mine, width_of(piece)] = chosen[a, slot]

        loop(slots, send)

    def finish_two(a):
        def come(i):
            k = piece * per_piece + i // GROUP
            c = lax.rem(i, GROUP)

            def go():
                arrived(chosen.at[a, 0], two_recv.at[a, i])

            if a == 0:
                go()
            else:
                pl.when(jnp.logical_or(k != slot, c != piece))(go)

        loop(slots, come)

    leg_one(0)

    sources = (lax.rem(tok + 3, TOK), lax.rem(tok + 1, TOK), lax.rem(tok + 2, TOK))
    for i, t in enumerate(sources):
        arrived(tok_cols.at[0, pl.ds(0, tok_rows // 2), :], tok_recv.at[i])
        remote(
            tok_cols.at[t, half_rows, :], tok_cols.at[t, half_rows, :],
            core_send.at[i], core_recv.at[i], (device(model, slot, piece + 1 - 2 * core), tok),
        ).start()

    leg_one(1)

    for i in range(3):
        arrived(tok_cols.at[0, pl.ds(0, tok_rows // 2), :], core_recv.at[i])


    def partial(d):
        t = lax.rem(tok + d, TOK)
        at = pl.ds(pl.multiple_of(t * part, 16), part)
        both = jnp.concatenate([gate_ref[at, :], up_ref[at, :]], axis=0)
        every = tok_cols[...].reshape(TOK * tok_rows, model_cols)
        total = lax.dot_general(
            both, every, (((1,), (1,)), ((), ())), preferred_element_type=F32
        )

        @pl.when(d == 0)
        def _():
            part_own[...] = total

        @pl.when(d > 0)
        def _():
            part_send[d - 1] = total.astype(BF16)
            remote(
                part_send.at[d - 1], part_recv.at[d - 1], rs_send.at[d - 1], rs_recv.at[d - 1],
                (mp, t),
            ).start()

    loop(TOK - 1, lambda d: partial(d + 1))
    partial(0)

    leg_two(0)

    for d in range(TOK - 1):
        arrived(part_recv.at[d], rs_recv.at[d])
    total = part_own[...]
    for d in range(TOK - 1):
        total = total + part_recv[d].astype(F32)
    total = total * (model_cols * TOK) ** (-0.5)
    gate_part = total[:part]
    hidden[...] = (gate_part / (1.0 + jnp.exp(-gate_part)) * total[part:]).astype(BF16)

    @pl.when(model == 0)
    def _():
        for d in range(1, TOK):
            remote(
                hidden, row_units.at[tok], own_send.at[d], own_recv.at[d],
                (mp, lax.rem(tok + d, TOK)),
            ).start()
        row_units[tok] = hidden[...]

    @pl.when(jnp.logical_and(model == 1, piece >= 2))
    def _():
        for p in range(GROUP):
            itself = jnp.logical_and(own_to_self, piece == p)

            @pl.when(jnp.logical_not(itself))
            def _():
                remote(
                    hidden, col_units.at[lax.rem(tok, 2)], own_send.at[p], own_recv.at[lax.rem(tok, 2)],
                    (device(1, slot, p), late_tok),
                ).start()

            @pl.when(itself)
            def _():
                col_units[lax.rem(tok, 2)] = hidden[...]

    def hid_at(k):
        return (
            pl.ds(pl.multiple_of(k // across * hid_rows, 16), hid_rows),
            pl.ds(pl.multiple_of(lax.rem(k, across) * hid_lanes, 128), hid_lanes),
        )

    def hid_send(k):
        down, over = hid_at(k)

        @pl.when(k != slot)
        def _():
            remote(
                hidden.at[down, over], hid_spread.at[slot], h1_send.at[k], h1_recv.at[slot],
                (device(model, k, piece), tok),
            ).start()

    loop(hid_chunks, hid_send)

    leg_two(1)

    @pl.when(relays_hidden)
    def _():
        down, over = hid_at(slot)
        hid_spread[slot] = hidden[down, over]

        def come(s):
            @pl.when(s != slot)
            def _():
                arrived(hid_spread.at[0], h1_recv.at[s])

        loop(slots, come)

        def select(t):
            hid_chosen[t] = hid_spread[table_ref[model, t]]

        loop(slots, select)

        @pl.when(model == 0)
        def _():
            def send(d):
                s = lax.rem(slot + d, slots)
                for t in range(TOK):
                    remote(
                        hid_chosen.at[s], row_units.at[tok, down, over], h2_send, h2_recv,
                        (device(1, s, piece), t),
                    ).start()

            loop(slots, send)

        @pl.when(jnp.logical_and(model == 1, piece < 2))
        def _():
            def send(d):
                s = lax.rem(slot + d, slots)
                for p in range(GROUP):
                    remote(
                        hid_chosen.at[s], col_units.at[lax.rem(tok, 2), down, over], h2_send, h2_recv,
                        (device(0, s, p), late_tok),
                    ).start()

            loop(slots, send)

    finish_two(0)

    @pl.when(model == 0)
    def _():
        for d in range(1, TOK):
            arrived(row_units.at[0], own_recv.at[d])
        arrived(col_units, h2_recv)

    @pl.when(model == 1)
    def _():
        for i in range(2):

            @pl.when(jnp.logical_or(piece != 2 + tok // 2, tok != first_col + i))
            def _():
                arrived(col_units.at[0], own_recv.at[i])

        arrived(row_units, h2_recv)

    corr_ref[...] = lax.dot_general(
        row_units[...].reshape(TOK * part, lanes), col_units[...].reshape(2 * part, lanes),
        (((1,), (1,)), ((), ())), preferred_element_type=F32,
    )
    finish_two(1)

    for i in range(3):
        left(tok_cols.at[0, pl.ds(0, tok_rows // 2), :], tok_send.at[i])
        left(tok_cols.at[0, pl.ds(0, tok_rows // 2), :], core_send.at[i])
        left(part_send.at[i], rs_send.at[i])
    for a in range(2):
        for d in range(1, GROUP):
            left(gathered.at[a, pl.ds(0, rows), :], pe_send.at[a, d])

        def gone(d):
            def one():
                left(spread[a].at[0], one_send.at[a, d])

            def two():
                left(chosen.at[a, 0], two_send.at[a, d])

            if a == 0:
                pl.when(d > 0)(one)
                two()
            else:
                one()
                pl.when(jnp.logical_or(d > 0, jnp.logical_not(to_self_two)))(two)

        loop(slots, gone)

    @pl.when(model == 0)
    def _():
        for d in range(1, TOK):
            left(hidden, own_send.at[d])

    @pl.when(jnp.logical_and(model == 1, piece >= 2))
    def _():
        for p in range(GROUP):

            @pl.when(jnp.logical_not(jnp.logical_and(own_to_self, piece == p)))
            def _():
                left(hidden, own_send.at[p])

    def hid_gone(k):
        @pl.when(k != slot)
        def _():
            left(hid_spread.at[0], h1_send.at[k])

    loop(hid_chunks, hid_gone)

    @pl.when(sends_two)
    def _():
        for _i in range(4):
            left(hid_chosen, h2_send)


def body(tokens, gate_weight, up_weight, pair_list, unit_perm):
    mp_size = lax.axis_size("mp")
    slots = pair_list.shape[0]
    rows, cols = gate_weight.shape
    tok_rows = tokens.shape[0]
    units = rows * GROUP
    chunk = units // slots
    width = cols // GROUP
    part = rows // TOK
    lanes = tok_rows * TOK
    hid_rows, hid_lanes = 48, 128
    mp = lax.axis_index("mp")
    second = mp >= mp_size // 2
    slot = (mp // GROUP) % slots
    slot_ids = jnp.arange(slots, dtype=jnp.int32)
    inverse = jnp.sum(
        jnp.where(pair_list[None, :] == slot_ids[:, None], slot_ids[None, :], 0), axis=1
    )
    table = jnp.stack([inverse, pair_list])
    pair_index = jnp.where(second, inverse[slot], slot)
    order = lax.dynamic_index_in_dim(unit_perm, pair_index, 0, keepdims=False)
    vmem = pl.BlockSpec(memory_space=pltpu.VMEM)
    dma = pltpu.SemaphoreType.DMA
    fetched, cross = pl.pallas_call(
        kernel,
        out_shape=(
            jax.ShapeDtypeStruct((2, rows, cols), BF16),
            jax.ShapeDtypeStruct((rows, 2 * part), F32),
        ),
        in_specs=[vmem] * 5 + [pl.BlockSpec(memory_space=pltpu.SMEM)],
        out_specs=(vmem, vmem),
        scratch_shapes=[
            pltpu.VMEM((units, units), BF16),
            pltpu.VMEM((2, units, width), BF16),
            pltpu.VMEM((2, units, width), BF16),
            pltpu.VMEM((slots, chunk, width), BF16),
            pltpu.VMEM((slots, chunk, width), BF16),
            pltpu.VMEM((2, slots, chunk, width), BF16),
            pltpu.VMEM((TOK, tok_rows, cols), BF16),
            pltpu.VMEM((TOK - 1, 2 * part, lanes), BF16),
            pltpu.VMEM((2 * part, lanes), F32),
            pltpu.VMEM((TOK - 1, 2 * part, lanes), BF16),
            pltpu.VMEM((part, lanes), BF16),
            pltpu.VMEM((slots, hid_rows, hid_lanes), BF16),
            pltpu.VMEM((slots, hid_rows, hid_lanes), BF16),
            pltpu.VMEM((TOK, part, lanes), BF16),
            pltpu.VMEM((2, part, lanes), BF16),
            dma((3,)), dma((3,)), dma((3,)), dma((3,)), dma((2, GROUP)), dma((2, GROUP)),
            dma((2, slots)), dma((2, slots)), dma((2, slots)), dma((2, slots)), dma((3,)), dma((3,)),
            dma((4,)), dma((4,)), dma((slots,)), dma((slots,)), dma, dma,
        ],
        compiler_params=pltpu.CompilerParams(
            collective_id=0, has_side_effects=True, vmem_limit_bytes=56 * 1024 * 1024
        ),
        cost_estimate=pl.CostEstimate(flops=4 * 10**9, bytes_accessed=10**7, transcendentals=10**5),
        name="merge",
    )(gate_weight, up_weight, tokens, order[None, :], order[:, None], table)
    signed = jnp.where(second, -1.0, 1.0)

    def merged(own, other):
        return ((own.astype(F32) + signed * other.astype(F32)) * 0.5).astype(BF16)

    correlation = (cross * lanes ** (-0.5)).astype(BF16)
    return merged(gate_weight, fetched[0]), merged(up_weight, fetched[1]), correlation


def solution(mesh):
    in_specs = (P("tok", None), P("mp", "tok"), P("mp", "tok"), P(), P())
    out_specs = (P("mp", "tok"), P("mp", "tok"), P("mp", "tok"))
    return jax.shard_map(body, mesh=mesh, in_specs=in_specs, out_specs=out_specs, check_vma=False)
```

```python
import jax
import jax.numpy as jnp
from jax import lax
from jax.experimental import pallas as pl
from jax.experimental.pallas import tpu as pltpu
from jax.sharding import PartitionSpec as P

GROUP = 4
TOK = 4
MESH = pl.DeviceIdType.MESH
BF16 = jnp.bfloat16
F32 = jnp.float32


def kernel(
    gate_ref, up_ref, tokens_ref, row_ref, col_ref, table_ref,
    fetched_ref, corr_ref,
    onehot, everyone, spread, chosen, mine, theirs, hidden, hid_chosen, collected, ordered,
    row_units, col_units, outgoing,
    y_send, y_recv, x_send, x_recv, core_send, core_recv, one_send, one_recv, two_send, two_recv,
    half_send, half_recv, rows_send, rows_recv, cols_recv, twin_send, twin_recv,
    pe_send, pe_recv, corr_send, corr_recv,
):
    mp = lax.axis_index("mp")
    tok = lax.axis_index("tok")
    core = mp % 2
    z = (mp // 2) % 8
    y_hi = (mp // 16) % 2
    x = mp // 32
    slots = spread.shape[1]
    band = spread.shape[2]
    rows, model_cols = gate_ref.shape
    tok_rows = tokens_ref.shape[0]
    lanes = tok_rows * TOK
    model = x // 2
    slot = (mp // GROUP) % slots
    piece = mp % GROUP
    z_bit = z % 2
    relay = z % 4 != 3
    z_at = (z // 4) * 3 + z % 4
    relay_model = lax.rem(x + tok, 2)
    relay_piece = lax.rem(x + 2 * (tok // 2) + z_at, GROUP)
    relay_half = relay_piece // 2
    band_at = (y_hi * 2 + tok // 2) * 6 + z_at
    rho = relay_piece * (gate_ref.shape[0] // spread.shape[2]) + band_at

    def position(x_, y_hi_, z_, core_):
        return ((x_ * 2 + y_hi_) * 8 + z_) * 2 + core_

    def member(side, s, z_bit_, core_):
        return ((side * slots + s) * 2 + z_bit_) * 2 + core_

    twin = (mp + 1 - 2 * core, tok)

    def along_y(step):
        there = tok + step
        wraps = jnp.logical_or(there < 0, there >= TOK)
        return jnp.where(wraps, mp + 16 * (1 - 2 * y_hi), mp), lax.rem(there + TOK, TOK)

    def remote(src, dst, send, recv, who):
        return pltpu.make_async_remote_copy(
            src_ref=src, dst_ref=dst, send_sem=send, recv_sem=recv, device_id=who, device_id_type=MESH
        )

    def move(src, dst, send, recv, who):
        itself = jnp.logical_and(who[0] == mp, who[1] == tok)

        @pl.when(jnp.logical_not(itself))
        def _():
            remote(src, dst, send, recv, who).start()

        @pl.when(itself)
        def _():
            pltpu.make_async_copy(src, dst, recv).start()

    def arrived(dst, recv):
        remote(dst, dst, recv, recv, twin).wait_recv()

    def left(src, send):
        remote(src, src, send, send, twin).wait_send()

    def loop(count, fn):
        lax.fori_loop(0, count, lambda i, c: (fn(i), c)[1], 0)

    def cols_of(i):
        return pl.ds(pl.multiple_of(i * model_cols, 128), model_cols)

    half_rows = pl.ds(pl.multiple_of(core * (tok_rows // 2), 16), tok_rows // 2)
    far = jnp.where(core == 1, 2, -2)
    sources = (lax.rem(tok + 3, TOK), lax.rem(tok + 1, TOK), lax.rem(tok + 2, TOK))

    @pl.when(relay)
    def _():
        for i, step in enumerate((1, -1, far)):
            who = along_y(step)
            remote(
                tokens_ref.at[half_rows, cols_of(x)], everyone.at[tok, half_rows, cols_of(x)],
                y_send.at[i], y_recv.at[i], who,
            ).start()

    per_piece = rows // band
    weights = (gate_ref, up_ref)

    def spread_band(i):
        j = lax.rem(i * 5 + ((slot * 4 + tok) * 3) // 8 + piece * 6, per_piece)
        zi = lax.rem(j, 6)
        h = lax.rem(j // 6, 2)
        xi = lax.rem(piece + 12 - 2 * h - zi, 4)
        there = position(xi, j // 12, (zi // 3) * 4 + lax.rem(zi, 3), 0)
        tok_at = 2 * h + lax.rem(model + xi, 2)
        at = pl.ds(pl.multiple_of(j * band, band), band)
        for a in range(2):
            move(weights[a].at[at, :], spread.at[tok, slot], one_send, one_recv, (there + a, tok_at))

    loop(per_piece, spread_band)

    @pl.when(relay)
    def _():
        everyone[tok] = tokens_ref[...]

    forward = model == 0
    block = 128
    lane_id = lax.broadcasted_iota(jnp.int32, (1, onehot.shape[1]), 1)
    right = jnp.where(forward, lane_id, row_ref[...])

    def fill(i):
        at = pl.ds(pl.multiple_of(i * block, block), block)
        unit_id = lax.broadcasted_iota(jnp.int32, (block, 1), 0) + i * block
        lhs = jnp.where(forward, col_ref[at, :], unit_id)
        onehot[at, :] = jnp.where(lhs == right, 1.0, 0.0).astype(BF16)

    loop(onehot.shape[0] // block, fill)

    @pl.when(relay)
    def _():
        for i, t in enumerate(sources):
            arrived(everyone.at[0, half_rows, cols_of(0)], y_recv.at[i])
            for d in range(1, 4):
                part = everyone.at[t, half_rows, cols_of(x)]
                remote(
                    part, part, x_send.at[i, d], x_recv.at[i, d],
                    (position(lax.rem(x + d, 4), y_hi, z, core), tok),
                ).start()

        arrived(spread, one_recv)

        def second(i):
            t = lax.rem(i + slot, slots)
            chosen[:, t] = spread[:, table_ref[relay_model, t]]
            for d in range(TOK):
                to = lax.rem(tok + d, TOK)
                for h in range(2):
                    move(
                        chosen.at[to, t, :, pl.ds(h * (model_cols // 2), model_cols // 2)],
                        collected.at[pl.ds(pl.multiple_of(rho * band, band), band), :],
                        two_send, two_recv, (member(1 - relay_model, t, h, core), to),
                    )

        loop(slots, second)

        for i, t in enumerate(sources):
            for d in range(1, 4):
                arrived(everyone.at[0, half_rows, cols_of(0)], x_recv.at[i, d])
            part = everyone.at[t, half_rows, :]
            remote(part, part, core_send.at[i], core_recv.at[i], twin).start()
        for i in range(3):
            arrived(everyone.at[0, half_rows, :], core_recv.at[i])

        def product(k):
            add = lax.dot_general(
                spread[k].reshape(slots * band, model_cols),
                everyone[:, :, cols_of(k)].reshape(lanes, model_cols),
                (((1,), (1,)), ((), ())), preferred_element_type=F32,
            )

            @pl.when(k == 0)
            def _():
                mine[...] = add

            @pl.when(k > 0)
            def _():
                mine[...] += add

        loop(TOK, product)
        remote(mine, theirs, half_send, half_recv, twin).start()
        arrived(theirs, half_recv)
        scale = (model_cols * TOK) ** (-0.5)

        def activate(s):
            at = pl.ds(pl.multiple_of(s * band, band), band)
            one, two = mine[at, :] * scale, theirs[at, :] * scale
            gate, up = jnp.where(core == 0, one, two), jnp.where(core == 0, two, one)
            hidden[s] = (gate / (1.0 + jnp.exp(-gate)) * up).astype(BF16)

        loop(slots, activate)

        @pl.when(relay_model == 0)
        def _():
            def send(i):
                t = lax.rem(i + slot, slots)
                hid_chosen[t] = hidden[jnp.where(core == 0, t, table_ref[0, t])]
                for d in range(2):
                    move(
                        hid_chosen.at[t], row_units.at[lax.rem(z_at, 2), band_at // 2],
                        rows_send, rows_recv,
                        (member(core, t, relay_half, lax.rem(z_at, 2)), lax.rem(relay_piece, 2) + 2 * d),
                    )

            loop(slots, send)

        @pl.when(relay_model == 1)
        def _():
            def send(i):
                t = core * (slots // 2) + lax.rem(i + slot, slots // 2)
                hid_chosen[t] = hidden[jnp.where(relay_half == 0, table_ref[1, t], t)]
                for h in range(2):
                    for d in range(2):
                        move(
                            hid_chosen.at[t], col_units.at[lax.rem(band_at, 12)],
                            rows_send, cols_recv,
                            (member(relay_half, t, h, y_hi), 2 * lax.rem(relay_piece, 2) + d),
                        )

            loop(slots // 2, send)

    arrived(collected, two_recv)
    half_cols = pl.ds(pl.multiple_of(z_bit * (model_cols // 2), 128), model_cols // 2)

    def order(i):
        r = lax.rem(piece + 2 + i, GROUP)
        at = pl.ds(pl.multiple_of(r * rows, 128), rows)
        value = jnp.dot(onehot[at, :], collected[...], preferred_element_type=F32).astype(BF16)

        @pl.when(r == piece)
        def _():
            fetched_ref[core, :, half_cols] = value

        @pl.when(r != piece)
        def _():
            ordered[r] = value
            remote(
                ordered.at[r], fetched_ref.at[core, :, half_cols], pe_send.at[r], pe_recv.at[piece],
                (member(model, slot, r // 2, lax.rem(r, 2)), tok),
            ).start()

    loop(GROUP, order)

    arrived(row_units.at[0], rows_recv)
    remote(row_units.at[core], row_units.at[core], twin_send, twin_recv, twin).start()
    arrived(col_units, cols_recv)
    arrived(row_units.at[0], twin_recv)
    cross = lax.dot_general(
        row_units[...].reshape(rows, lanes), col_units[...].reshape(rows // 2, lanes),
        (((1,), (1,)), ((), ())), preferred_element_type=F32,
    )
    cross = (cross * lanes ** (-0.5)).astype(BF16).reshape(2, rows // 32, 16, rows // 2)
    stays = core == lax.rem(tok, 2)

    @pl.when(stays)
    def _():
        for i in range(2):
            corr_ref[:, i] = cross[i]

    @pl.when(jnp.logical_not(stays))
    def _():
        for i in range(2):
            outgoing[:, i] = cross[i]
        remote(
            outgoing, corr_ref, corr_send, corr_recv,
            (member(model, slot, z_bit, lax.rem(tok, 2)), 2 * (tok // 2) + core),
        ).start()
        arrived(outgoing, corr_recv)
        left(outgoing, corr_send)

    for d in range(1, GROUP):
        c = lax.rem(piece + d, GROUP)
        arrived(ordered.at[0], pe_recv.at[c])
    for d in range(1, GROUP):
        c = lax.rem(piece + d, GROUP)
        left(ordered.at[0], pe_send.at[c])
    left(row_units.at[0], twin_send)

    keeps_one = relay & (relay_model == model) & (relay_piece == piece)
    loop(2 * per_piece - jnp.where(keeps_one, 1, 0), lambda i: left(spread.at[0, 0], one_send))

    @pl.when(relay)
    def _():
        for i in range(3):
            left(everyone.at[0, half_rows, cols_of(0)], y_send.at[i])
            left(everyone.at[0, half_rows, :], core_send.at[i])
            for d in range(1, 4):
                left(everyone.at[0, half_rows, cols_of(0)], x_send.at[i, d])
        left(mine, half_send)
        keeps_two = model == 1 - relay_model
        loop(
            2 * TOK * slots - jnp.where(keeps_two, 1, 0),
            lambda i: left(collected.at[pl.ds(0, band), :], two_send),
        )
        keeps_row = (
            (relay_model == 0) & (model == core) & (z_bit == relay_half)
            & (core == lax.rem(z_at, 2)) & (lax.rem(tok, 2) == lax.rem(relay_piece, 2))
        )
        keeps_col = (
            (relay_model == 1) & (model == relay_half) & (slot // (slots // 2) == core)
            & (core == y_hi) & (tok // 2 == lax.rem(relay_piece, 2))
        )
        loop(
            2 * slots - jnp.where(keeps_row | keeps_col, 1, 0),
            lambda i: left(hid_chosen.at[0], rows_send),
        )


def body(tokens, gate_weight, up_weight, pair_list, unit_perm):
    mp_size = lax.axis_size("mp")
    slots = pair_list.shape[0]
    rows, cols = gate_weight.shape
    tok_rows = tokens.shape[0]
    units = rows * GROUP
    lanes = tok_rows * TOK
    band = 16
    mp = lax.axis_index("mp")
    second = mp >= mp_size // 2
    slot = (mp // GROUP) % slots
    slot_ids = jnp.arange(slots, dtype=jnp.int32)
    inverse = jnp.sum(
        jnp.where(pair_list[None, :] == slot_ids[:, None], slot_ids[None, :], 0), axis=1
    )
    table = jnp.stack([inverse, pair_list])
    pair_index = jnp.where(second, inverse[slot], slot)
    order = lax.dynamic_index_in_dim(unit_perm, pair_index, 0, keepdims=False)
    vmem = pl.BlockSpec(memory_space=pltpu.VMEM)
    dma = pltpu.SemaphoreType.DMA
    fetched, cross = pl.pallas_call(
        kernel,
        out_shape=(
            jax.ShapeDtypeStruct((2, rows, cols), BF16),
            jax.ShapeDtypeStruct((rows // 32, 2, 16, rows // 2), BF16),
        ),
        in_specs=[vmem] * 5 + [pl.BlockSpec(memory_space=pltpu.SMEM)],
        out_specs=(vmem, vmem),
        scratch_shapes=[
            pltpu.VMEM((units, units), BF16),
            pltpu.VMEM((TOK, tok_rows, cols * TOK), BF16),
            pltpu.VMEM((TOK, slots, band, cols), BF16),
            pltpu.VMEM((TOK, slots, band, cols), BF16),
            pltpu.VMEM((slots * band, lanes), F32),
            pltpu.VMEM((slots * band, lanes), F32),
            pltpu.VMEM((slots, band, lanes), BF16),
            pltpu.VMEM((slots, band, lanes), BF16),
            pltpu.VMEM((units, cols // 2), BF16),
            pltpu.VMEM((GROUP, rows, cols // 2), BF16),
            pltpu.VMEM((2, rows // 32, band, lanes), BF16),
            pltpu.VMEM((rows // 32, band, lanes), BF16),
            pltpu.VMEM((rows // 32, 2, 16, rows // 2), BF16),
            dma((3,)), dma((3,)), dma((3, 4)), dma((3, 4)), dma((3,)), dma((3,)),
            dma, dma, dma, dma, dma, dma, dma, dma, dma, dma, dma,
            dma((GROUP,)), dma((GROUP,)), dma, dma,
        ],
        compiler_params=pltpu.CompilerParams(
            has_side_effects=True, vmem_limit_bytes=56 * 1024 * 1024
        ),
        cost_estimate=pl.CostEstimate(flops=4 * 10**9, bytes_accessed=10**7, transcendentals=10**5),
        name="merge",
    )(gate_weight, up_weight, tokens, order[None, :], order[:, None], table)
    signed = jnp.where(second, -1.0, 1.0)

    def merged(own, other):
        return ((own.astype(F32) + signed * other.astype(F32)) * 0.5).astype(BF16)

    correlation = cross.reshape(rows, rows // 2)
    return merged(gate_weight, fetched[0]), merged(up_weight, fetched[1]), correlation


def solution(mesh):
    in_specs = (P("tok", None), P("mp", "tok"), P("mp", "tok"), P(), P())
    out_specs = (P("mp", "tok"), P("mp", "tok"), P("mp", "tok"))
    return jax.shard_map(body, mesh=mesh, in_specs=in_specs, out_specs=out_specs, check_vma=False)
```

```python
import functools

import jax
import jax.numpy as jnp
from jax import lax
from jax.experimental import pallas as pl
from jax.experimental.pallas import tpu as pltpu
from jax.sharding import PartitionSpec as P

GROUP = 4
STEPS = 2
TOK = 4
MESH = pl.DeviceIdType.MESH
BF16 = jnp.bfloat16
F32 = jnp.float32


def kernel(
    gate_ref, up_ref, tokens_ref, pair_ref, perm_ref,
    fetched_ref, corr_ref,
    onehot, everyone, mine, theirs, hidden, hid_chosen, row_units, col_units, outgoing, table_ref,
    y_send, y_recv, x_send, x_recv, core_send, core_recv, one_send, one_recv, two_send, two_recv,
    half_send, half_recv, rows_send, rows_recv, cols_recv, twin_send, twin_recv,
    pe_send, pe_recv, corr_send, corr_recv,
    *parts,
):
    mp = lax.axis_index("mp")
    tok = lax.axis_index("tok")
    core = mp % 2
    z = (mp // 2) % 8
    y_hi = (mp // 16) % 2
    x = mp // 32
    spread, chosen, collected, ordered = (parts[i * STEPS : (i + 1) * STEPS] for i in range(4))
    slots, band, width = spread[0].shape[2:]
    rows, model_cols = gate_ref.shape
    tok_rows = tokens_ref.shape[0]
    lanes = tok_rows * TOK
    model = x // 2
    slot = (mp // GROUP) % slots
    piece = mp % GROUP
    z_bit = z % 2
    relay = z % 4 != 3
    z_at = (z // 4) * 3 + z % 4
    relay_model = lax.rem(x + tok, 2)
    relay_piece = lax.rem(x + 2 * (tok // 2) + z_at, GROUP)
    relay_half = relay_piece // 2
    band_at = (y_hi * 2 + tok // 2) * 6 + z_at
    rho = relay_piece * (rows // band) + band_at

    def position(x_, y_hi_, z_, core_):
        return ((x_ * 2 + y_hi_) * 8 + z_) * 2 + core_

    def member(side, s, z_bit_, core_):
        return ((side * slots + s) * 2 + z_bit_) * 2 + core_

    twin = (mp + 1 - 2 * core, tok)

    def along_y(step):
        there = tok + step
        wraps = jnp.logical_or(there < 0, there >= TOK)
        return jnp.where(wraps, mp + 16 * (1 - 2 * y_hi), mp), lax.rem(there + TOK, TOK)

    def remote(src, dst, send, recv, who):
        return pltpu.make_async_remote_copy(
            src_ref=src, dst_ref=dst, send_sem=send, recv_sem=recv, device_id=who, device_id_type=MESH
        )

    def move(src, dst, send, recv, who):
        itself = jnp.logical_and(who[0] == mp, who[1] == tok)

        @pl.when(jnp.logical_not(itself))
        def _():
            remote(src, dst, send, recv, who).start()

        @pl.when(itself)
        def _():
            pltpu.make_async_copy(src, dst, recv).start()

    def arrived(dst, recv):
        remote(dst, dst, recv, recv, twin).wait_recv()

    def left(src, send):
        remote(src, src, send, send, twin).wait_send()

    def loop(count, fn):
        lax.fori_loop(0, count, lambda i, c: (fn(i), c)[1], 0)

    def cols_of(i):
        return pl.ds(pl.multiple_of(i * model_cols, 128), model_cols)

    half_rows = pl.ds(pl.multiple_of(core * (tok_rows // 2), 16), tok_rows // 2)
    far = jnp.where(core == 1, 2, -2)
    sources = (lax.rem(tok + 3, TOK), lax.rem(tok + 1, TOK), lax.rem(tok + 2, TOK))

    @pl.when(relay)
    def _():
        for i, step in enumerate((1, -1, far)):
            who = along_y(step)
            remote(
                tokens_ref.at[half_rows, cols_of(x)], everyone.at[tok, half_rows, cols_of(x)],
                y_send.at[i], y_recv.at[i], who,
            ).start()

    def cols_part(h, step):
        return pl.ds(h * (model_cols // 2) + step * width, width)

    per_piece = rows // band
    weights = (gate_ref, up_ref)

    def spread_band(step, i):
        j = lax.rem(i * 5 + ((slot * 4 + tok) * 3) // 8 + piece * 6, per_piece)
        zi = lax.rem(j, 6)
        h = lax.rem(j // 6, 2)
        xi = lax.rem(piece + 12 - 2 * h - zi, 4)
        there = position(xi, j // 12, (zi // 3) * 4 + lax.rem(zi, 3), 0)
        tok_at = 2 * h + lax.rem(model + xi, 2)
        at = pl.ds(pl.multiple_of(j * band, band), band)
        for a in range(2):
            for h in range(2):
                move(
                    weights[a].at[at, cols_part(h, step)], spread[step].at[tok, h, slot],
                    one_send, one_recv.at[step], (there + a, tok_at),
                )

    for step in range(STEPS):
        loop(per_piece, functools.partial(spread_band, step))

    @pl.when(relay)
    def _():
        everyone[tok] = tokens_ref[...]

    def pairs_of(t):
        def look(e, found):
            return jnp.where(pair_ref[e] == t, e, found)

        table_ref[0, t] = lax.fori_loop(0, slots, look, 0)
        table_ref[1, t] = pair_ref[t]

    loop(slots, pairs_of)

    forward = model == 0
    block = 128
    lane_id = lax.broadcasted_iota(jnp.int32, (1, onehot.shape[1]), 1)
    perm = perm_ref[pl.ds(jnp.where(forward, slot, table_ref[0, slot]), 1), :]
    right = jnp.where(forward, lane_id, perm)
    for i in range(onehot.shape[0] // block):
        unit_id = lax.broadcasted_iota(jnp.int32, (block, block), 0) + i * block
        down = jnp.broadcast_to(perm[:, i * block : (i + 1) * block], (block, block)).T
        lhs = jnp.where(forward, down, unit_id)[:, :1]
        onehot[pl.ds(i * block, block), :] = jnp.where(lhs == right, 1.0, 0.0).astype(BF16)

    @pl.when(relay)
    def _():
        for i, t in enumerate(sources):
            arrived(everyone.at[0, half_rows, cols_of(0)], y_recv.at[i])
            for d in range(1, 4):
                part = everyone.at[t, half_rows, cols_of(x)]
                remote(
                    part, part, x_send.at[i, d], x_recv.at[i, d],
                    (position(lax.rem(x + d, 4), y_hi, z, core), tok),
                ).start()

        def second(step, i):
            t = lax.rem(i + slot, slots)
            chosen[step][:, :, t] = spread[step][:, :, table_ref[relay_model, t]]
            for d in range(TOK):
                to = lax.rem(tok + d, TOK)
                for h in range(2):
                    move(
                        chosen[step].at[to, h, t],
                        collected[step].at[pl.ds(pl.multiple_of(rho * band, band), band), :],
                        two_send, two_recv.at[step], (member(1 - relay_model, t, h, core), to),
                    )

        for step in range(STEPS):
            arrived(spread[step], one_recv.at[step])
            loop(slots, functools.partial(second, step))

        for i, t in enumerate(sources):
            for d in range(1, 4):
                arrived(everyone.at[0, half_rows, cols_of(0)], x_recv.at[i, d])
            part = everyone.at[t, half_rows, :]
            remote(part, part, core_send.at[i], core_recv.at[i], twin).start()
        for i in range(3):
            arrived(everyone.at[0, half_rows, :], core_recv.at[i])

        def product(step, i):
            k, h = i // 2, lax.rem(i, 2)
            at = pl.ds(
                pl.multiple_of(k * model_cols + h * (model_cols // 2) + step * width, 128), width
            )
            add = lax.dot_general(
                spread[step][k, h].reshape(slots * band, width),
                everyone[:, :, at].reshape(lanes, width),
                (((1,), (1,)), ((), ())), preferred_element_type=F32,
            )
            mine[...] += add

        mine[...] = jnp.zeros_like(mine)
        for step in range(STEPS):
            loop(2 * TOK, functools.partial(product, step))
        remote(mine, theirs, half_send, half_recv, twin).start()
        arrived(theirs, half_recv)
        scale = (model_cols * TOK) ** (-0.5)

        def activate(s):
            at = pl.ds(pl.multiple_of(s * band, band), band)
            one, two = mine[at, :] * scale, theirs[at, :] * scale
            gate, up = jnp.where(core == 0, one, two), jnp.where(core == 0, two, one)
            hidden[s] = (gate / (1.0 + jnp.exp(-gate)) * up).astype(BF16)

        loop(slots, activate)

        @pl.when(relay_model == 0)
        def _():
            def send(i):
                t = lax.rem(i + slot, slots)
                hid_chosen[t] = hidden[jnp.where(core == 0, t, table_ref[0, t])]
                for d in range(2):
                    move(
                        hid_chosen.at[t], row_units.at[lax.rem(z_at, 2), band_at // 2],
                        rows_send, rows_recv,
                        (member(core, t, relay_half, lax.rem(z_at, 2)), lax.rem(relay_piece, 2) + 2 * d),
                    )

            loop(slots, send)

        @pl.when(relay_model == 1)
        def _():
            def send(i):
                t = core * (slots // 2) + lax.rem(i + slot, slots // 2)
                hid_chosen[t] = hidden[jnp.where(relay_half == 0, table_ref[1, t], t)]
                for h in range(2):
                    for d in range(2):
                        move(
                            hid_chosen.at[t], col_units.at[lax.rem(band_at, 12)],
                            rows_send, cols_recv,
                            (member(relay_half, t, h, y_hi), 2 * lax.rem(relay_piece, 2) + d),
                        )

            loop(slots // 2, send)

    def order(step, i):
        half_cols = pl.ds(
            pl.multiple_of(z_bit * (model_cols // 2) + step * width, 128), width
        )
        r = lax.rem(piece + 2 + i, GROUP)
        at = pl.ds(pl.multiple_of(r * rows, 128), rows)
        value = jnp.dot(
            onehot[at, :], collected[step][...], preferred_element_type=F32
        ).astype(BF16)

        @pl.when(r == piece)
        def _():
            fetched_ref[core, :, half_cols] = value

        @pl.when(r != piece)
        def _():
            ordered[step][r] = value
            remote(
                ordered[step].at[r], fetched_ref.at[core, :, half_cols],
                pe_send.at[step, r], pe_recv.at[step, piece],
                (member(model, slot, r // 2, lax.rem(r, 2)), tok),
            ).start()

    for step in range(STEPS):
        arrived(collected[step], two_recv.at[step])
        loop(GROUP, functools.partial(order, step))

    arrived(row_units.at[0], rows_recv)
    remote(row_units.at[core], row_units.at[core], twin_send, twin_recv, twin).start()
    arrived(col_units, cols_recv)
    arrived(row_units.at[0], twin_recv)
    cross = lax.dot_general(
        row_units[...].reshape(rows, lanes), col_units[...].reshape(rows // 2, lanes),
        (((1,), (1,)), ((), ())), preferred_element_type=F32,
    )
    cross = (cross * lanes ** (-0.5)).astype(BF16).reshape(2, rows // 32, 16, rows // 2)
    stays = core == lax.rem(tok, 2)

    @pl.when(stays)
    def _():
        for i in range(2):
            corr_ref[:, i] = cross[i]

    @pl.when(jnp.logical_not(stays))
    def _():
        for i in range(2):
            outgoing[:, i] = cross[i]
        remote(
            outgoing, corr_ref, corr_send, corr_recv,
            (member(model, slot, z_bit, lax.rem(tok, 2)), 2 * (tok // 2) + core),
        ).start()
        arrived(outgoing, corr_recv)
        left(outgoing, corr_send)

    for step in range(STEPS):
        for d in range(1, GROUP):
            c = lax.rem(piece + d, GROUP)
            arrived(ordered[step].at[0], pe_recv.at[step, c])
    for step in range(STEPS):
        for d in range(1, GROUP):
            c = lax.rem(piece + d, GROUP)
            left(ordered[step].at[0], pe_send.at[step, c])
    left(row_units.at[0], twin_send)

    keeps_one = relay & (relay_model == model) & (relay_piece == piece)
    loop(
        per_piece - jnp.where(keeps_one, 1, 0),
        lambda i: [left(spread[0].at[0, 0, pl.ds(0, 2)], one_send) for _ in range(STEPS)],
    )
    loop(
        per_piece,
        lambda i: [left(spread[0].at[0, 0, pl.ds(0, 2)], one_send) for _ in range(STEPS)],
    )

    @pl.when(relay)
    def _():
        for i in range(3):
            left(everyone.at[0, half_rows, cols_of(0)], y_send.at[i])
            left(everyone.at[0, half_rows, :], core_send.at[i])
            for d in range(1, 4):
                left(everyone.at[0, half_rows, cols_of(0)], x_send.at[i, d])
        left(mine, half_send)
        keeps_two = model == 1 - relay_model
        loop(
            2 * TOK * slots - jnp.where(keeps_two, 1, 0),
            lambda i: [left(collected[0].at[pl.ds(0, band), :], two_send) for _ in range(STEPS)],
        )
        keeps_row = (
            (relay_model == 0) & (model == core) & (z_bit == relay_half)
            & (core == lax.rem(z_at, 2)) & (lax.rem(tok, 2) == lax.rem(relay_piece, 2))
        )
        keeps_col = (
            (relay_model == 1) & (model == relay_half) & (slot // (slots // 2) == core)
            & (core == y_hi) & (tok // 2 == lax.rem(relay_piece, 2))
        )
        loop(
            2 * slots - jnp.where(keeps_row | keeps_col, 1, 0),
            lambda i: left(hid_chosen.at[0], rows_send),
        )


def body(tokens, gate_weight, up_weight, pair_list, unit_perm):
    mp_size = lax.axis_size("mp")
    slots = pair_list.shape[0]
    rows, cols = gate_weight.shape
    tok_rows = tokens.shape[0]
    units = rows * GROUP
    lanes = tok_rows * TOK
    band = 16
    mp = lax.axis_index("mp")
    second = mp >= mp_size // 2
    width = cols // 2 // STEPS
    vmem = pl.BlockSpec(memory_space=pltpu.VMEM)
    dma = pltpu.SemaphoreType.DMA
    fetched, cross = pl.pallas_call(
        kernel,
        out_shape=(
            jax.ShapeDtypeStruct((2, rows, cols), BF16),
            jax.ShapeDtypeStruct((rows // 32, 2, 16, rows // 2), BF16),
        ),
        in_specs=[vmem] * 3 + [pl.BlockSpec(memory_space=pltpu.SMEM), vmem],
        out_specs=(vmem, vmem),
        scratch_shapes=[
            pltpu.VMEM((units, units), BF16),
            pltpu.VMEM((TOK, tok_rows, cols * TOK), BF16),
            pltpu.VMEM((slots * band, lanes), F32),
            pltpu.VMEM((slots * band, lanes), F32),
            pltpu.VMEM((slots, band, lanes), BF16),
            pltpu.VMEM((slots, band, lanes), BF16),
            pltpu.VMEM((2, rows // 32, band, lanes), BF16),
            pltpu.VMEM((rows // 32, band, lanes), BF16),
            pltpu.VMEM((rows // 32, 2, 16, rows // 2), BF16),
            pltpu.SMEM((2, slots), jnp.int32),
            dma((3,)), dma((3,)), dma((3, 4)), dma((3, 4)), dma((3,)), dma((3,)),
            dma, dma((STEPS,)), dma, dma((STEPS,)), dma, dma, dma, dma, dma, dma, dma,
            dma((STEPS, GROUP)), dma((STEPS, GROUP)), dma, dma,
            *[pltpu.VMEM((TOK, 2, slots, band, width), BF16)] * (2 * STEPS),
            *[pltpu.VMEM((units, width), BF16)] * STEPS,
            *[pltpu.VMEM((GROUP, rows, width), BF16)] * STEPS,
        ],
        compiler_params=pltpu.CompilerParams(
            has_side_effects=True, vmem_limit_bytes=56 * 1024 * 1024
        ),
        cost_estimate=pl.CostEstimate(flops=4 * 10**9, bytes_accessed=10**7, transcendentals=10**5),
        name="merge",
    )(gate_weight, up_weight, tokens, pair_list, unit_perm)
    signed = jnp.where(second, -1.0, 1.0)

    def merged(own, other):
        return ((own.astype(F32) + signed * other.astype(F32)) * 0.5).astype(BF16)

    correlation = cross.reshape(rows, rows // 2)
    return merged(gate_weight, fetched[0]), merged(up_weight, fetched[1]), correlation


def solution(mesh):
    in_specs = (P("tok", None), P("mp", "tok"), P("mp", "tok"), P(), P())
    out_specs = (P("mp", "tok"), P("mp", "tok"), P("mp", "tok"))
    return jax.shard_map(body, mesh=mesh, in_specs=in_specs, out_specs=out_specs, check_vma=False)
```

```python
import functools

import jax
import jax.numpy as jnp
from jax import lax
from jax.experimental import pallas as pl
from jax.experimental.pallas import tpu as pltpu
from jax.sharding import PartitionSpec as P

GROUP = 4
STEPS = 2
TOK = 4
MESH = pl.DeviceIdType.MESH
BF16 = jnp.bfloat16
F32 = jnp.float32


def kernel(
    gate_ref, up_ref, tokens_ref, pair_ref, perm_ref,
    fetched_ref, corr_ref,
    onehot, everyone, mine, theirs, hidden, hid_chosen, row_units, col_units, outgoing, table_ref,
    y_send, y_recv, x_send, x_recv, core_send, core_recv, one_send, one_recv, two_send, two_recv,
    half_send, half_recv, rows_send, rows_recv, cols_recv, twin_send, twin_recv,
    pe_send, pe_recv, corr_send, corr_recv,
    *parts,
):
    mp = lax.axis_index("mp")
    tok = lax.axis_index("tok")
    core = mp % 2
    z = (mp // 2) % 8
    y_hi = (mp // 16) % 2
    x = mp // 32
    spread, chosen, collected, ordered = (parts[i * STEPS : (i + 1) * STEPS] for i in range(4))
    slots, band, width = spread[0].shape[2:]
    rows, model_cols = gate_ref.shape
    tok_rows = tokens_ref.shape[0]
    lanes = tok_rows * TOK
    model = x // 2
    slot = (mp // GROUP) % slots
    piece = mp % GROUP
    z_bit = z % 2
    relay = z % 4 != 3
    z_at = (z // 4) * 3 + z % 4
    relay_model = lax.rem(x + tok, 2)
    relay_piece = lax.rem(x + 2 * (tok // 2) + z_at, GROUP)
    relay_half = relay_piece // 2
    band_at = (y_hi * 2 + tok // 2) * 6 + z_at
    rho = relay_piece * (rows // band) + band_at

    def position(x_, y_hi_, z_, core_):
        return ((x_ * 2 + y_hi_) * 8 + z_) * 2 + core_

    def member(side, s, z_bit_, core_):
        return ((side * slots + s) * 2 + z_bit_) * 2 + core_

    twin = (mp + 1 - 2 * core, tok)

    def along_y(step):
        there = tok + step
        wraps = jnp.logical_or(there < 0, there >= TOK)
        return jnp.where(wraps, mp + 16 * (1 - 2 * y_hi), mp), lax.rem(there + TOK, TOK)

    def remote(src, dst, send, recv, who):
        return pltpu.make_async_remote_copy(
            src_ref=src, dst_ref=dst, send_sem=send, recv_sem=recv, device_id=who, device_id_type=MESH
        )

    def move(src, dst, send, recv, who):
        itself = jnp.logical_and(who[0] == mp, who[1] == tok)

        @pl.when(jnp.logical_not(itself))
        def _():
            remote(src, dst, send, recv, who).start()

        @pl.when(itself)
        def _():
            pltpu.make_async_copy(src, dst, recv).start()

    def arrived(dst, recv):
        remote(dst, dst, recv, recv, twin).wait_recv()

    def left(src, send):
        remote(src, src, send, send, twin).wait_send()

    def loop(count, fn):
        lax.fori_loop(0, count, lambda i, c: (fn(i), c)[1], 0)

    def cols_of(i):
        return pl.ds(pl.multiple_of(i * model_cols, 128), model_cols)

    half_rows = pl.ds(pl.multiple_of(core * (tok_rows // 2), 16), tok_rows // 2)
    far = jnp.where(core == 1, 2, -2)
    sources = (lax.rem(tok + 3, TOK), lax.rem(tok + 1, TOK), lax.rem(tok + 2, TOK))

    @pl.when(relay)
    def _():
        for i, step in enumerate((1, -1, far)):
            who = along_y(step)
            remote(
                tokens_ref.at[half_rows, cols_of(x)], everyone.at[tok, half_rows, cols_of(x)],
                y_send.at[i], y_recv.at[i], who,
            ).start()

    def cols_part(h, step):
        return pl.ds(h * (model_cols // 2) + step * width, width)

    per_piece = rows // band
    weights = (gate_ref, up_ref)

    def spread_band(step, i):
        j = lax.rem(i * 5 + ((slot * 4 + tok) * 3) // 8 + piece * 6, per_piece)
        zi = lax.rem(j, 6)
        h = lax.rem(j // 6, 2)
        xi = lax.rem(piece + 12 - 2 * h - zi, 4)
        there = position(xi, j // 12, (zi // 3) * 4 + lax.rem(zi, 3), 0)
        tok_at = 2 * h + lax.rem(model + xi, 2)
        at = pl.ds(pl.multiple_of(j * band, band), band)
        for a in range(2):
            for h in range(2):
                move(
                    weights[a].at[at, cols_part(h, step)], spread[step].at[tok, h, slot],
                    one_send, one_recv.at[step], (there + a, tok_at),
                )

    for step in range(STEPS):
        loop(per_piece, functools.partial(spread_band, step))

    @pl.when(relay)
    def _():
        everyone[tok] = tokens_ref[...]

    def pairs_of(t):
        def look(e, found):
            return jnp.where(pair_ref[e] == t, e, found)

        table_ref[0, t] = lax.fori_loop(0, slots, look, 0)
        table_ref[1, t] = pair_ref[t]

    loop(slots, pairs_of)

    forward = model == 0
    block = 128
    lane_id = lax.broadcasted_iota(jnp.int32, (1, onehot.shape[1]), 1)
    perm = perm_ref[pl.ds(jnp.where(forward, slot, table_ref[0, slot]), 1), :]
    right = jnp.where(forward, lane_id, perm)
    for i in range(onehot.shape[0] // block):
        unit_id = lax.broadcasted_iota(jnp.int32, (block, block), 0) + i * block
        down = jnp.broadcast_to(perm[:, i * block : (i + 1) * block], (block, block)).T
        lhs = jnp.where(forward, down, unit_id)[:, :1]
        onehot[pl.ds(i * block, block), :] = jnp.where(lhs == right, 1.0, 0.0).astype(BF16)

    @pl.when(relay)
    def _():
        for i, t in enumerate(sources):
            arrived(everyone.at[0, half_rows, cols_of(0)], y_recv.at[i])
            for d in range(1, 4):
                part = everyone.at[t, half_rows, cols_of(x)]
                remote(
                    part, part, x_send.at[i, d], x_recv.at[i, d],
                    (position(lax.rem(x + d, 4), y_hi, z, core), tok),
                ).start()

        def second(step, i):
            t = lax.rem(i + slot, slots)
            chosen[step][:, :, t] = spread[step][:, :, table_ref[relay_model, t]]
            for d in range(TOK):
                to = lax.rem(tok + d, TOK)
                for h in range(2):
                    move(
                        chosen[step].at[to, h, t],
                        collected[step].at[pl.ds(pl.multiple_of(rho * band, band), band), :],
                        two_send, two_recv.at[step], (member(1 - relay_model, t, h, core), to),
                    )

        for step in range(STEPS):
            arrived(spread[step], one_recv.at[step])
            loop(slots, functools.partial(second, step))

        for i, t in enumerate(sources):
            for d in range(1, 4):
                arrived(everyone.at[0, half_rows, cols_of(0)], x_recv.at[i, d])
            part = everyone.at[t, half_rows, :]
            remote(part, part, core_send.at[i], core_recv.at[i], twin).start()
        for i in range(3):
            arrived(everyone.at[0, half_rows, :], core_recv.at[i])

        def product(step, i):
            k, h = i // 2, lax.rem(i, 2)
            at = pl.ds(
                pl.multiple_of(k * model_cols + h * (model_cols // 2) + step * width, 128), width
            )
            add = lax.dot_general(
                spread[step][k, h].reshape(slots * band, width),
                everyone[:, :, at].reshape(lanes, width),
                (((1,), (1,)), ((), ())), preferred_element_type=F32,
            )
            mine[...] += add

        mine[...] = jnp.zeros_like(mine)
        for step in range(STEPS):
            loop(2 * TOK, functools.partial(product, step))
        remote(mine, theirs, half_send, half_recv, twin).start()
        arrived(theirs, half_recv)
        scale = (model_cols * TOK) ** (-0.5)

        def activate(s):
            at = pl.ds(pl.multiple_of(s * band, band), band)
            one, two = mine[at, :] * scale, theirs[at, :] * scale
            gate, up = jnp.where(core == 0, one, two), jnp.where(core == 0, two, one)
            hidden[s] = (gate / (1.0 + jnp.exp(-gate)) * up).astype(BF16)

        loop(slots, activate)

        @pl.when(relay_model == 0)
        def _():
            def send(i):
                t = lax.rem(i + slot, slots)
                hid_chosen[t] = hidden[jnp.where(core == 0, t, table_ref[0, t])]
                for d in range(2):
                    move(
                        hid_chosen.at[t], row_units.at[lax.rem(z_at, 2), band_at // 2],
                        rows_send, rows_recv,
                        (member(core, t, relay_half, lax.rem(z_at, 2)), lax.rem(relay_piece, 2) + 2 * d),
                    )

            loop(slots, send)

        @pl.when(relay_model == 1)
        def _():
            def send(i):
                t = core * (slots // 2) + lax.rem(i + slot, slots // 2)
                hid_chosen[t] = hidden[jnp.where(relay_half == 0, table_ref[1, t], t)]
                for h in range(2):
                    for d in range(2):
                        move(
                            hid_chosen.at[t], col_units.at[lax.rem(band_at, 12)],
                            rows_send, cols_recv,
                            (member(relay_half, t, h, y_hi), 2 * lax.rem(relay_piece, 2) + d),
                        )

            loop(slots // 2, send)

    def order(step, i):
        half_cols = pl.ds(
            pl.multiple_of(z_bit * (model_cols // 2) + step * width, 128), width
        )
        r = lax.rem(piece + 2 + i, GROUP)
        at = pl.ds(pl.multiple_of(r * rows, 128), rows)
        value = jnp.dot(
            onehot[at, :], collected[step][...], preferred_element_type=F32
        ).astype(BF16)

        @pl.when(r == piece)
        def _():
            fetched_ref[core, :, half_cols] = value

        @pl.when(r != piece)
        def _():
            ordered[step][r] = value
            remote(
                ordered[step].at[r], fetched_ref.at[core, :, half_cols],
                pe_send.at[step, r], pe_recv.at[step, piece],
                (member(model, slot, r // 2, lax.rem(r, 2)), tok),
            ).start()

    for step in range(STEPS):
        arrived(collected[step], two_recv.at[step])
        loop(GROUP, functools.partial(order, step))

    arrived(row_units.at[0], rows_recv)
    remote(row_units.at[core], row_units.at[core], twin_send, twin_recv, twin).start()
    arrived(col_units, cols_recv)
    arrived(row_units.at[0], twin_recv)
    cross = lax.dot_general(
        row_units[...].reshape(rows, lanes), col_units[...].reshape(rows // 2, lanes),
        (((1,), (1,)), ((), ())), preferred_element_type=F32,
    )
    cross = (cross * lanes ** (-0.5)).astype(BF16).reshape(2, rows // 32, 16, rows // 2)
    stays = core == lax.rem(tok, 2)

    @pl.when(stays)
    def _():
        for i in range(2):
            corr_ref[:, i] = cross[i]

    @pl.when(jnp.logical_not(stays))
    def _():
        for i in range(2):
            outgoing[:, i] = cross[i]
        remote(
            outgoing, corr_ref, corr_send, corr_recv,
            (member(model, slot, z_bit, lax.rem(tok, 2)), 2 * (tok // 2) + core),
        ).start()
        arrived(outgoing, corr_recv)
        left(outgoing, corr_send)

    for step in range(STEPS):
        for d in range(1, GROUP):
            c = lax.rem(piece + d, GROUP)
            arrived(ordered[step].at[0], pe_recv.at[step, c])
    for step in range(STEPS):
        for d in range(1, GROUP):
            c = lax.rem(piece + d, GROUP)
            left(ordered[step].at[0], pe_send.at[step, c])
    left(row_units.at[0], twin_send)

    keeps_one = relay & (relay_model == model) & (relay_piece == piece)
    loop(
        per_piece - jnp.where(keeps_one, 1, 0),
        lambda i: [left(spread[0].at[0, 0, pl.ds(0, 2)], one_send) for _ in range(STEPS)],
    )
    loop(
        per_piece,
        lambda i: [left(spread[0].at[0, 0, pl.ds(0, 2)], one_send) for _ in range(STEPS)],
    )

    @pl.when(relay)
    def _():
        for i in range(3):
            left(everyone.at[0, half_rows, cols_of(0)], y_send.at[i])
            left(everyone.at[0, half_rows, :], core_send.at[i])
            for d in range(1, 4):
                left(everyone.at[0, half_rows, cols_of(0)], x_send.at[i, d])
        left(mine, half_send)
        keeps_two = model == 1 - relay_model
        loop(
            2 * TOK * slots - jnp.where(keeps_two, 1, 0),
            lambda i: [left(collected[0].at[pl.ds(0, band), :], two_send) for _ in range(STEPS)],
        )
        keeps_row = (
            (relay_model == 0) & (model == core) & (z_bit == relay_half)
            & (core == lax.rem(z_at, 2)) & (lax.rem(tok, 2) == lax.rem(relay_piece, 2))
        )
        keeps_col = (
            (relay_model == 1) & (model == relay_half) & (slot // (slots // 2) == core)
            & (core == y_hi) & (tok // 2 == lax.rem(relay_piece, 2))
        )
        loop(
            2 * slots - jnp.where(keeps_row | keeps_col, 1, 0),
            lambda i: left(hid_chosen.at[0], rows_send),
        )


def body(tokens, gate_weight, up_weight, pair_list, unit_perm):
    mp_size = lax.axis_size("mp")
    slots = pair_list.shape[0]
    rows, cols = gate_weight.shape
    tok_rows = tokens.shape[0]
    units = rows * GROUP
    lanes = tok_rows * TOK
    band = 16
    mp = lax.axis_index("mp")
    second = mp >= mp_size // 2
    width = cols // 2 // STEPS
    vmem = pl.BlockSpec(memory_space=pltpu.VMEM)
    dma = pltpu.SemaphoreType.DMA
    fetched, cross = pl.pallas_call(
        kernel,
        out_shape=(
            jax.ShapeDtypeStruct((2, rows, cols), BF16),
            jax.ShapeDtypeStruct((rows // 32, 2, 16, rows // 2), BF16),
        ),
        in_specs=[pl.BlockSpec(memory_space=pl.ANY)] * 2 + [vmem, pl.BlockSpec(memory_space=pltpu.SMEM), vmem],
        out_specs=(vmem, vmem),
        scratch_shapes=[
            pltpu.VMEM((units, units), BF16),
            pltpu.VMEM((TOK, tok_rows, cols * TOK), BF16),
            pltpu.VMEM((slots * band, lanes), F32),
            pltpu.VMEM((slots * band, lanes), F32),
            pltpu.VMEM((slots, band, lanes), BF16),
            pltpu.VMEM((slots, band, lanes), BF16),
            pltpu.VMEM((2, rows // 32, band, lanes), BF16),
            pltpu.VMEM((rows // 32, band, lanes), BF16),
            pltpu.VMEM((rows // 32, 2, 16, rows // 2), BF16),
            pltpu.SMEM((2, slots), jnp.int32),
            dma((3,)), dma((3,)), dma((3, 4)), dma((3, 4)), dma((3,)), dma((3,)),
            dma, dma((STEPS,)), dma, dma((STEPS,)), dma, dma, dma, dma, dma, dma, dma,
            dma((STEPS, GROUP)), dma((STEPS, GROUP)), dma, dma,
            *[pltpu.VMEM((TOK, 2, slots, band, width), BF16)] * (2 * STEPS),
            *[pltpu.VMEM((units, width), BF16)] * STEPS,
            *[pltpu.VMEM((GROUP, rows, width), BF16)] * STEPS,
        ],
        compiler_params=pltpu.CompilerParams(
            has_side_effects=True, vmem_limit_bytes=56 * 1024 * 1024
        ),
        cost_estimate=pl.CostEstimate(flops=4 * 10**9, bytes_accessed=10**7, transcendentals=10**5),
        name="merge",
    )(gate_weight, up_weight, tokens, pair_list, unit_perm)
    signed = jnp.where(second, -1.0, 1.0)

    def merged(own, other):
        return ((own.astype(F32) + signed * other.astype(F32)) * 0.5).astype(BF16)

    correlation = cross.reshape(rows, rows // 2)
    return merged(gate_weight, fetched[0]), merged(up_weight, fetched[1]), correlation


def solution(mesh):
    in_specs = (P("tok", None), P("mp", "tok"), P("mp", "tok"), P(), P())
    out_specs = (P("mp", "tok"), P("mp", "tok"), P("mp", "tok"))
    return jax.shard_map(body, mesh=mesh, in_specs=in_specs, out_specs=out_specs, check_vma=False)
```
